32 devices in a mesh: grp: 2 (over y), rep: 4 (over x, core), tp: 4 (over z).
Axes of the slice: x: 2, y: 2, z: 4, core: 2. Of those that a mesh axis runs over, the one named last changes fastest.
Arguments:
- query: bfloat16 [512, 2, 8192], P(('grp', 'rep'), None, 'tp'), parts along dimension 0, may hold values from -8 to 8
- kv_pool: bfloat16 [2, 1280, 128, 8, 128], P(None, ('grp', 'rep'), None, 'tp'), parts along dimension 1, may hold values from -6 to 6, as said below
- ctx_len: int32 [512], P(('grp', 'rep')), parts along dimension 0, may hold values from 1 to 510, as said below
- migrations: int32 [8, 8, 3], P(('grp', 'rep')), parts along dimension 0, may hold values from 0 to 63, as said below
- o_weight: bfloat16 [8192, 8192], P('tp'), may hold values from -0.5 to 0.5
Outputs:
- layer_out: bfloat16 [512, 2, 8192], P(('grp', 'rep')), parts along dimension 0
- arrived_pages: bfloat16 [2, 256, 128, 8, 128], P(None, ('grp', 'rep'), None, 'tp'), parts along dimension 1
The draws below stay inside these ranges and needn't reach their ends.
There are 2 independent parts, one for each index of `grp`. The reference program is written for one: setup_inputs(seed, part) draws one part's arguments, and reference() takes and returns one part's arrays. A program takes and returns all parts, laid end to end along the dimension named above; an argument that names none is the same for every part. Nothing has to cross between parts.
Inputs may be any that keep to these rules, and one draw needn't show every extreme that they name: For every replica, the page counts ceil((ctx_len + 2) / 128) of its 64 requests sum to at most 160, and its requests' pages lie in its pool in request order from its first page on. `migrations`: row q holds 8 entries (slot of a request on replica q, destination replica, pages moved). Half of the replicas each migrate 8 distinct requests, each with all its pages, which are exactly 4, to one destination among the other half, and each of those receives from exactly one replica; the rows of the other replicas are (0, q, 0) and they send nothing. `kv_pool`: head copies j and k hold equal values when j == k.
All inputs are finite; a program needn't handle non-finite values.
Results may differ from the reference program's by a relative error of at most 0.0054.
Values may be sent and summed in bfloat16 or wider, within the bound.
A program may use at most 512 MiB of HBM per device.

```python
import math
import jax
import jax.numpy as jnp
from jax import lax

D = 8192
HEADS = 64
KV_HEADS = 8
HD = 128
PAGE = 128
MAXP = 4
STEPS = 2
SLOTS = 64
MIG = 8
POOL = 160
REQUESTS = 256
KV_REP = 1
KV_SLOTS = 8
N_REP = 4


def request_layout(key):
    half_count = N_REP // 2
    replica_order = jax.random.permutation(jax.random.fold_in(key, 101), N_REP).astype(jnp.int32)
    replica_rank = jnp.zeros((N_REP,), jnp.int32).at[replica_order].set(jnp.arange(N_REP, dtype=jnp.int32))
    is_busy = replica_rank < half_count
    slot_keys = jax.random.split(jax.random.fold_in(key, 102), N_REP)
    slot_perm = jax.vmap(lambda sub_key: jax.random.permutation(sub_key, SLOTS))(slot_keys).astype(jnp.int32)
    last_value = slot_perm[:, SLOTS - 1:SLOTS]
    slot_position = jnp.arange(SLOTS, dtype=jnp.int32)[None, :]
    slot_perm = jnp.where(slot_position == SLOTS - 1, 0, jnp.where(slot_perm == 0, last_value, slot_perm)).astype(jnp.int32)
    offsets = jax.random.randint(jax.random.fold_in(key, 103), (N_REP, SLOTS), 1, PAGE - 1).astype(jnp.int32)
    busy_pages = MAXP - slot_perm % MAXP
    busy_length = (busy_pages - 1) * PAGE + jnp.where(slot_perm == 0, PAGE - 2, offsets)
    spare_length = jnp.where(slot_perm == 0, 1, offsets)
    lengths = jnp.where(is_busy[:, None], busy_length, spare_length).astype(jnp.int32)
    inverse = jnp.argsort(slot_perm, axis=1).astype(jnp.int32)
    picked = inverse[:, ::MAXP][:, :MIG]
    partner = replica_order[jnp.minimum(replica_rank + half_count, N_REP - 1)]
    own_index = jnp.arange(N_REP, dtype=jnp.int32)
    destination = jnp.where(is_busy, partner, own_index)
    slot_field = jnp.where(is_busy[:, None], picked, 0)
    dest_field = jnp.broadcast_to(destination[:, None], (N_REP, MIG))
    count_field = jnp.broadcast_to(jnp.where(is_busy, MAXP, 0)[:, None], (N_REP, MIG))
    migration_lists = jnp.stack([slot_field, dest_field, count_field], axis=-1).astype(jnp.int32)
    return (lengths.reshape(-1), migration_lists)


def draw_ctx_len(key, part):
    lengths, migration_lists = request_layout(key)
    return lengths


def draw_migrations(key, part):
    lengths, migration_lists = request_layout(key)
    return migration_lists


def draw_query(key, part):
    key = jax.random.fold_in(key, 7)
    shape = (REQUESTS, STEPS, HEADS * HD)
    drawn = jnp.clip(jax.random.normal(key, shape, jnp.float32), -6.0, 6.0)
    return drawn.astype(jnp.bfloat16)


def draw_kv_pool(key, part):
    key = jax.random.fold_in(key, 9)
    shape = (2, N_REP * POOL, PAGE, KV_HEADS, HD)
    drawn = jnp.clip(jax.random.normal(key, shape, jnp.float32), -5.0, 5.0)
    return jnp.repeat(drawn.astype(jnp.bfloat16), KV_REP, axis=3)


def steps_of(rng, shape, cuts, least, largest):
    factor_of = 1.0
    for axis_at, blocks in cuts:
        draws = jax.random.uniform(jax.random.fold_in(jax.random.fold_in(rng, 6), axis_at), (blocks,), jnp.float32, least / len(cuts), largest / len(cuts))
        factor_of = factor_of * jnp.repeat(jnp.exp(draws), shape[axis_at] // blocks).reshape((-1,) + (1,) * (len(shape) - 1 - axis_at))
    return factor_of


def scatter_about(key, extent, deviation, most, shards=(), kind=jnp.bfloat16):
    entries = jax.random.normal(key, extent, jnp.float32) * deviation
    if len(shards) > 0:
        entries = steps_of(key, extent, shards, -0.22, 0.18) * entries
    return jnp.clip(entries, min=-most, max=most).astype(kind)


def setup_inputs(seed: int = 0, part: int = 0) -> dict:
    key_of = jax.random.split(jax.random.key(seed), 6)
    part_keys = jax.random.split(jax.random.fold_in(key_of[5], part), 6)
    query = draw_query(jax.random.fold_in(jax.random.fold_in(key_of[5], part), 71), part)
    kv_pool = draw_kv_pool(jax.random.fold_in(jax.random.fold_in(key_of[5], part), 71), part)
    ctx_len = draw_ctx_len(jax.random.fold_in(jax.random.fold_in(key_of[5], part), 71), part)
    migrations = draw_migrations(jax.random.fold_in(jax.random.fold_in(key_of[5], part), 71), part)
    o_weight = scatter_about(key_of[4], (HEADS * HD, D), HD ** -0.5, 0.5, ((0, 4),))
    return {"query": query, "kv_pool": kv_pool, "ctx_len": ctx_len, "migrations": migrations, "o_weight": o_weight}


def reference(query, kv_pool, ctx_len, migrations, o_weight):
    score_scale = 1.0 / math.sqrt(HD)
    group_size = HEADS // KV_HEADS
    page_counts = (ctx_len + 2 + PAGE - 1) // PAGE
    per_replica = page_counts.reshape(N_REP, SLOTS)
    pool_base = (jnp.arange(N_REP, dtype=jnp.int32) * POOL)[:, None]
    starts = (jnp.cumsum(per_replica, axis=1) - per_replica + pool_base).astype(jnp.int32)
    first_pages = starts.reshape(-1)
    kv_heads_only = kv_pool[:, :, :, ::KV_REP, :]

    def one_request(inputs):
        first_page, context, row_query = inputs
        page_rows = jnp.minimum(first_page + jnp.arange(MAXP, dtype=jnp.int32), N_REP * POOL - 1).astype(jnp.int32)
        key_rows = kv_heads_only[0, page_rows].reshape(MAXP * PAGE, KV_HEADS, HD).astype(jnp.float32)
        values = kv_heads_only[1, page_rows].reshape(MAXP * PAGE, KV_HEADS, HD).astype(jnp.float32)
        queries = row_query.reshape(STEPS, KV_HEADS, group_size, HD).astype(jnp.float32)
        scores = jnp.einsum('skgd,tkd->skgt', queries, key_rows, precision=lax.Precision.HIGHEST) * score_scale
        positions = jnp.arange(MAXP * PAGE, dtype=jnp.int32)
        limits = context + 1 + jnp.arange(STEPS, dtype=jnp.int32)
        valid_keys = positions[None, :] < limits[:, None]
        scores = jnp.where(valid_keys[:, None, None, :], scores, -jnp.inf)
        row_top = lax.optimization_barrier(jnp.max(scores, axis=-1, keepdims=True))
        weights = jnp.exp(scores - row_top)
        normalizer = lax.optimization_barrier(jnp.sum(weights, axis=-1))
        rounded = lax.optimization_barrier(weights.astype(jnp.bfloat16)).astype(jnp.float32)
        mixed = jnp.einsum('skgt,tkd->skgd', rounded, values, precision=lax.Precision.HIGHEST)
        mixed = mixed / normalizer[..., None]
        return mixed.astype(jnp.bfloat16).reshape(STEPS, HEADS * HD)
    attention = lax.map(one_request, (first_pages, ctx_len, query))
    layer_out = jnp.dot(attention.reshape(REQUESTS * STEPS, HEADS * HD), o_weight, preferred_element_type=jnp.float32)
    layer_out = layer_out.astype(jnp.bfloat16).reshape(REQUESTS, STEPS, D)
    slot_field = migrations[:, :, 0]
    dest_field = migrations[:, :, 1]
    count_field = migrations[:, :, 2]
    first_moved = jnp.take_along_axis(starts, slot_field, axis=1)
    page_range = jnp.arange(MAXP, dtype=jnp.int32)
    moved_rows = jnp.minimum(first_moved[:, :, None] + page_range, N_REP * POOL - 1).astype(jnp.int32)
    moved_valid = (page_range[None, None, :] < count_field[:, :, None]).reshape(N_REP, MIG * MAXP)
    moved = kv_pool[:, moved_rows.reshape(-1)].reshape(2, N_REP, MIG * MAXP, PAGE, KV_SLOTS, HD)
    moved = jnp.where(moved_valid[None, :, :, None, None, None], moved, jnp.zeros((), jnp.bfloat16))
    dest_pages = jnp.repeat(dest_field, MAXP, axis=1)
    landed_blocks = []
    for receiver in range(N_REP):
        is_target = dest_pages == receiver
        picked = jnp.where(is_target[None, :, :, None, None, None], moved, jnp.zeros((), jnp.bfloat16))
        landed_blocks.append(lax.optimization_barrier(jnp.sum(picked.astype(jnp.float32), axis=1)).astype(jnp.bfloat16))
    arrived = jnp.stack(landed_blocks, axis=1).reshape(2, N_REP * MIG * MAXP, PAGE, KV_SLOTS, HD)
    return (layer_out, arrived)
```

```python
import functools
import itertools
import math

import jax
import jax.numpy as jnp
from jax import lax
from jax.experimental import pallas as pl
from jax.experimental.pallas import tpu as pltpu
from jax.sharding import PartitionSpec as P

MAXP = 4
MESH = pl.DeviceIdType.MESH
VMEM_BYTES = 60 * 1024 * 1024


def divisor_near(total, most):
    for parts in range(min(most, total), 0, -1):
        if total % parts == 0:
            return parts
    return 1


def gather_kernel(page_len, page_rows, ctx_ref, mig_ref, kv_ref, out_ref, zeros, sems):
    entries = mig_ref.shape[1]
    span = MAXP * page_rows
    zeros[...] = jnp.zeros_like(zeros)
    last = kv_ref.shape[1] - span

    def first_row(slot):
        def add(i, total):
            return total + (ctx_ref[i] + 2 + page_len - 1) // page_len

        return lax.fori_loop(0, slot, add, 0) * page_rows

    for e in range(entries):
        moves = mig_ref[0, e, 2] > 0
        row = jnp.minimum(first_row(mig_ref[0, e, 0]), last)

        @pl.when(moves)
        def _():
            for c in range(2):
                pltpu.make_async_copy(
                    kv_ref.at[c, pl.ds(pl.multiple_of(row, page_rows), span)],
                    out_ref.at[c, pl.ds(e * span, span)],
                    sems.at[c, e],
                ).start()

        @pl.when(jnp.logical_not(moves))
        def _():
            for c in range(2):
                pltpu.make_async_copy(
                    zeros, out_ref.at[c, pl.ds(e * span, span)], sems.at[c, e]
                ).start()

    for e in range(entries):
        for c in range(2):
            pltpu.make_async_copy(
                zeros, out_ref.at[c, pl.ds(e * span, span)], sems.at[c, e]
            ).wait()


def gather_pages(kv_rows, ctx_len, migrations, page_len, page_rows):
    entries = migrations.shape[1]
    hd = kv_rows.shape[2]
    return pl.pallas_call(
        functools.partial(gather_kernel, page_len, page_rows),
        out_shape=jax.ShapeDtypeStruct((2, entries * MAXP * page_rows, hd), kv_rows.dtype),
        in_specs=[
            pl.BlockSpec(memory_space=pltpu.SMEM),
            pl.BlockSpec(memory_space=pltpu.SMEM),
            pl.BlockSpec(memory_space=pl.ANY),
        ],
        out_specs=pl.BlockSpec(memory_space=pl.ANY),
        scratch_shapes=[
            pltpu.VMEM((MAXP * page_rows, hd), kv_rows.dtype),
            pltpu.SemaphoreType.DMA((2, entries)),
        ],
        compiler_params=pltpu.CompilerParams(vmem_limit_bytes=VMEM_BYTES),
        name="gather_pages",
    )(ctx_len, migrations, kv_rows)


def attend_kernel(
    page_len, kv_slots, group, steps, chunks, together,
    ctx_ref, q_ref, kv_ref, out_ref, pool, starts, sems,
):
    requests, rows, hd = q_ref.shape
    page_rows = page_len * kv_slots
    pool_rows = kv_ref.shape[1]
    chunk_rows = pool_rows // chunks
    span = MAXP * page_rows
    last = pool_rows - span
    scale = 1.0 / math.sqrt(hd)

    def chunk_copy(c, i):
        part = pl.ds(pl.multiple_of(i * chunk_rows, chunk_rows), chunk_rows)
        return pltpu.make_async_copy(kv_ref.at[c, part], pool.at[c, part], sems.at[c, i])

    for i in range(chunks):
        for c in range(2):
            chunk_copy(c, i).start()

    def place(i, total):
        starts[i] = total
        return total + (ctx_ref[i] + 2 + page_len - 1) // page_len * page_rows

    lax.fori_loop(0, requests, place, 0)

    def wait_chunk(i, carry):
        for c in range(2):
            chunk_copy(c, i).wait()
        return carry

    row_id = lax.broadcasted_iota(jnp.int32, (rows, span), 0)
    column = lax.broadcasted_iota(jnp.int32, (rows, span), 1)
    per_step = kv_slots * group
    step_of = row_id // per_step
    same_head = (row_id % per_step) // group == column % kv_slots
    column = column - step_of * kv_slots

    def batch(b, waited):
        tail = jnp.minimum(starts[b * together + together - 1], last) + span
        needed = (tail + chunk_rows - 1) // chunk_rows
        lax.fori_loop(waited, needed, wait_chunk, 0)
        for u in range(together):
            r = b * together + u
            start = starts[r]
            base = pl.multiple_of(jnp.minimum(start, last), page_rows)
            low = start - base
            high = low + (ctx_ref[r] + 1) * kv_slots
            keys = pool[0, pl.ds(base, span), :]
            scores = lax.dot_general(
                q_ref[r], keys, (((1,), (1,)), ((), ())), preferred_element_type=jnp.float32
            ) * scale
            valid = same_head & (column + step_of * kv_slots >= low) & (column < high)
            scores = jnp.where(valid, scores, -1e30)
            top = jnp.max(scores, axis=1, keepdims=True)
            weights = jnp.exp(scores - top)
            total = jnp.sum(weights, axis=1, keepdims=True)
            values = pool[1, pl.ds(base, span), :]
            mixed = jnp.dot(
                weights.astype(jnp.bfloat16), values, preferred_element_type=jnp.float32
            )
            out_ref[r] = (mixed / total).astype(out_ref.dtype)
        return jnp.maximum(waited, needed)

    waited = lax.fori_loop(0, requests // together, batch, 0)
    lax.fori_loop(waited, chunks, wait_chunk, 0)


def attend(kv_rows, ctx_len, query, page_len, kv_slots):
    requests, steps, width = query.shape
    hd = kv_rows.shape[2]
    heads = width // hd
    group = heads // kv_slots
    rows = steps * heads
    pool_pages = kv_rows.shape[1] // (page_len * kv_slots)
    chunks = divisor_near(pool_pages, 16)
    together = divisor_near(requests, 4)
    shaped = query.reshape(requests, rows, hd)
    out = pl.pallas_call(
        functools.partial(attend_kernel, page_len, kv_slots, group, steps, chunks, together),
        out_shape=jax.ShapeDtypeStruct((requests, rows, hd), query.dtype),
        in_specs=[
            pl.BlockSpec(memory_space=pltpu.SMEM),
            pl.BlockSpec(memory_space=pltpu.VMEM),
            pl.BlockSpec(memory_space=pl.ANY),
        ],
        out_specs=pl.BlockSpec(memory_space=pltpu.VMEM),
        scratch_shapes=[
            pltpu.VMEM(kv_rows.shape, kv_rows.dtype),
            pltpu.SMEM((requests,), jnp.int32),
            pltpu.SemaphoreType.DMA((2, chunks)),
        ],
        compiler_params=pltpu.CompilerParams(vmem_limit_bytes=VMEM_BYTES),
        cost_estimate=pl.CostEstimate(
            flops=4 * requests * rows * MAXP * page_len * kv_slots * hd,
            bytes_accessed=2 * kv_rows.size,
            transcendentals=0,
        ),
        name="paged_attention",
    )(ctx_len, shaped, kv_rows)
    return out.reshape(requests * steps, width)


def project_kernel(
    count, chunks, slots, lag,
    a_ref, w_ref, out_ref,
    w_buf, own, staged, from_left, from_right,
    w_sem, send_left, send_right, recv_left, recv_right, cast_left, cast_right, cast_in,
):
    me = lax.axis_index("tp")
    width = w_buf.shape[2]
    has_left = me > 0
    has_right = me < count - 1
    left = jnp.maximum(me - 1, 0)
    right = jnp.minimum(me + 1, count - 1)

    def weights_copy(c):
        slot = lax.rem(c, slots)
        part = pl.ds(pl.multiple_of(c * width, width), width)
        return pltpu.make_async_copy(w_ref.at[:, part], w_buf.at[slot], w_sem.at[slot])

    def columns(c):
        return pl.ds(pl.multiple_of(c * width, width), width)

    def owner_of(c):
        return count // 2 - 1 + lax.rem(c, 2)

    def reduce_right(c):
        return pltpu.make_async_remote_copy(
            src_ref=staged.at[c], dst_ref=from_left.at[c],
            send_sem=send_right.at[c], recv_sem=recv_left.at[c],
            device_id={"tp": right}, device_id_type=MESH,
        )

    def reduce_left(c):
        return pltpu.make_async_remote_copy(
            src_ref=staged.at[c], dst_ref=from_right.at[c],
            send_sem=send_left.at[c], recv_sem=recv_right.at[c],
            device_id={"tp": left}, device_id_type=MESH,
        )

    def cast_to_right(c):
        return pltpu.make_async_remote_copy(
            src_ref=out_ref.at[:, columns(c)], dst_ref=out_ref.at[:, columns(c)],
            send_sem=cast_right.at[c], recv_sem=cast_in.at[c],
            device_id={"tp": right}, device_id_type=MESH,
        )

    def cast_to_left(c):
        return pltpu.make_async_remote_copy(
            src_ref=out_ref.at[:, columns(c)], dst_ref=out_ref.at[:, columns(c)],
            send_sem=cast_left.at[c], recv_sem=cast_in.at[c],
            device_id={"tp": left}, device_id_type=MESH,
        )

    for c in range(slots):
        weights_copy(c).start()

    barrier = pltpu.get_barrier_semaphore()

    @pl.when(has_left)
    def _():
        pl.semaphore_signal(barrier, inc=1, device_id={"tp": left}, device_id_type=MESH)

    @pl.when(has_right)
    def _():
        pl.semaphore_signal(barrier, inc=1, device_id={"tp": right}, device_id_type=MESH)

    pl.semaphore_wait(barrier, has_left.astype(jnp.int32) + has_right.astype(jnp.int32))

    def forward(c):
        owner = owner_of(c)

        @pl.when(me < owner)
        def _():
            cast_to_right(c).wait_recv()

            @pl.when(has_left)
            def _():
                cast_to_left(c).start()

        @pl.when(me > owner)
        def _():
            cast_to_left(c).wait_recv()

            @pl.when(has_right)
            def _():
                cast_to_right(c).start()

    def step(c, carry):
        slot = lax.rem(c, slots)
        owner = owner_of(c)
        weights_copy(c).wait()
        own[...] = jnp.dot(a_ref[...], w_buf[slot], preferred_element_type=jnp.float32)

        @pl.when(c + slots < chunks)
        def _():
            weights_copy(c + slots).start()

        @pl.when(has_left & (me <= owner))
        def _():
            reduce_right(c).wait_recv()
            own[...] = own[...] + from_left[c].astype(jnp.float32)

        @pl.when(has_right & (me >= owner))
        def _():
            reduce_left(c).wait_recv()
            own[...] = own[...] + from_right[c].astype(jnp.float32)

        @pl.when(me != owner)
        def _():
            staged[c] = own[...].astype(staged.dtype)

        @pl.when(me < owner)
        def _():
            reduce_right(c).start()

        @pl.when(me > owner)
        def _():
            reduce_left(c).start()

        @pl.when(me == owner)
        def _():
            out_ref[:, columns(c)] = own[...].astype(out_ref.dtype)

            @pl.when(has_left)
            def _():
                cast_to_left(c).start()

            @pl.when(has_right)
            def _():
                cast_to_right(c).start()

        @pl.when(c >= lag)
        def _():
            forward(c - lag)

        return carry

    lax.fori_loop(0, chunks, step, 0)

    def drain(c, carry):
        forward(c)
        return carry

    lax.fori_loop(chunks - lag, chunks, drain, 0)

    def finish(c, carry):
        owner = owner_of(c)

        @pl.when(me < owner)
        def _():
            reduce_right(c).wait_send()

        @pl.when(me > owner)
        def _():
            reduce_left(c).wait_send()

        @pl.when(has_left & (me <= owner))
        def _():
            cast_to_left(c).wait_send()

        @pl.when(has_right & (me >= owner))
        def _():
            cast_to_right(c).wait_send()

        return carry

    lax.fori_loop(0, chunks, finish, 0)


def project(attention, weight, count):
    rows, depth = attention.shape
    columns = weight.shape[1]
    width = 512 if columns % 512 == 0 else 128
    chunks = columns // width
    slots = min(4, chunks)
    lag = min(3, chunks)
    dma = pltpu.SemaphoreType.DMA
    return pl.pallas_call(
        functools.partial(project_kernel, count, chunks, slots, lag),
        out_shape=jax.ShapeDtypeStruct((rows, columns), attention.dtype),
        in_specs=[pl.BlockSpec(memory_space=pltpu.VMEM), pl.BlockSpec(memory_space=pl.ANY)],
        out_specs=pl.BlockSpec(memory_space=pltpu.VMEM),
        scratch_shapes=[
            pltpu.VMEM((slots, depth, width), weight.dtype),
            pltpu.VMEM((rows, width), jnp.float32),
            pltpu.VMEM((chunks, rows, width), attention.dtype),
            pltpu.VMEM((chunks, rows, width), attention.dtype),
            pltpu.VMEM((chunks, rows, width), attention.dtype),
            dma((slots,)),
        ]
        + [dma((chunks,))] * 7,
        compiler_params=pltpu.CompilerParams(
            collective_id=0, has_side_effects=True, vmem_limit_bytes=VMEM_BYTES
        ),
        cost_estimate=pl.CostEstimate(
            flops=2 * rows * depth * columns,
            bytes_accessed=2 * weight.size + 100 * 1000 * 1000,
            transcendentals=0,
        ),
        name="project_and_sum",
    )(attention, weight)


def on_device(query, kv_pool, ctx_len, migrations, o_weight):
    _, pool_size, page_len, kv_slots, hd = kv_pool.shape
    slot_count, step_count, _ = query.shape
    replicas = lax.axis_size("rep")
    count = lax.axis_size("tp")
    page_rows = page_len * kv_slots
    kv_rows = kv_pool.reshape(2, pool_size * page_rows, hd)
    outgoing = gather_pages(kv_rows, ctx_len, migrations, page_len, page_rows)
    lists = lax.all_gather(migrations[0, 0, 1:], ("grp", "rep"), axis=0)
    groups = lax.axis_size("grp")
    branch = branch_of(lists.reshape(groups, replicas, 2), groups, replicas)

    def serve(routes):
        def run(outgoing, kv_rows, ctx_len, query, o_weight):
            landed = lax.ppermute(outgoing, ("grp", "rep"), pairs_of(routes, replicas))
            attention = attend(kv_rows, ctx_len, query, page_len, kv_slots)
            return project(attention, o_weight, count), landed

        return run

    layer_out, landed = lax.switch(
        branch,
        [serve(routes) for routes in itertools.product(routes_of(replicas), repeat=groups)],
        outgoing, kv_rows, ctx_len, query, o_weight,
    )
    arrived = landed.reshape(2, -1, page_len, kv_slots, hd)
    return (layer_out.reshape(slot_count, step_count, -1), arrived)


def routes_of(replicas):
    routes = []
    for shift in range(1, replicas):
        routes.append([(i, i ^ shift) for i in range(replicas)])
        if shift > 1:
            for zero_sends in (0, 1):
                senders = (0 if zero_sends else shift, 1 ^ (shift if zero_sends else 0))
                routes.append([(i, i ^ shift) for i in senders])
    return routes


def branch_of(lists, groups, replicas):
    own = jnp.arange(replicas, dtype=jnp.int32)[None, :]
    sends = lists[:, :, 1] > 0
    shifts = jnp.max(jnp.where(sends, lists[:, :, 0] ^ own, 1), axis=1)
    zero = sends[:, 0].astype(jnp.int32)
    one = sends[:, 1].astype(jnp.int32)
    split = jnp.where((zero != one) & (shifts > 1), 1 + zero, 0)
    route = jnp.where(shifts == 1, 0, 3 * shifts - 5 + split)
    total = 3 * (replicas - 1) - 2
    index = jnp.int32(0)
    for g in range(groups):
        index = index * total + route[g]
    return index


def pairs_of(routes, replicas):
    return [
        (g * replicas + i, g * replicas + j) for g, route in enumerate(routes) for i, j in route
    ]


def solution(mesh):
    return jax.shard_map(
        on_device,
        mesh=mesh,
        in_specs=(
            P(("grp", "rep"), None, "tp"),
            P(None, ("grp", "rep"), None, "tp", None),
            P(("grp", "rep")),
            P(("grp", "rep"), None, None),
            P("tp", None),
        ),
        out_specs=(P(("grp", "rep"), None, None), P(None, ("grp", "rep"), None, "tp", None)),
        check_vma=False,
    )
```

```python
import functools
import math

import jax
import jax.numpy as jnp
from jax import lax
from jax.experimental import pallas as pl
from jax.experimental.pallas import tpu as pltpu
from jax.sharding import PartitionSpec as P

MAXP = 4
MESH = pl.DeviceIdType.MESH
VMEM_BYTES = 60 * 1024 * 1024


def divisor_near(total, most):
    for parts in range(min(most, total), 0, -1):
        if total % parts == 0:
            return parts
    return 1


def gather_kernel(page_len, page_rows, ctx_ref, mig_ref, kv_ref, *refs):
    outs, (held, in_sems, out_sems) = refs[:2], refs[2:]
    entries = mig_ref.shape[1]
    span = MAXP * page_rows
    last = kv_ref.shape[1] - span

    def first_row(slot):
        def add(i, total):
            return total + (ctx_ref[i] + 2 + page_len - 1) // page_len

        return lax.fori_loop(0, slot, add, 0) * page_rows

    def fetch(c, e, row):
        return pltpu.make_async_copy(
            kv_ref.at[c, pl.ds(pl.multiple_of(row, page_rows), span)],
            held.at[c, e],
            in_sems.at[c, e],
        )

    def store(c, e):
        return pltpu.make_async_copy(
            held.at[c, e], outs[c].at[pl.ds(e * span, span)], out_sems.at[c, e]
        )

    for e in range(entries):
        row = jnp.minimum(first_row(mig_ref[0, e, 0]), last)
        for c in range(2):
            fetch(c, e, row).start()
    for e in range(entries):
        moves = mig_ref[0, e, 2] > 0
        for c in range(2):
            fetch(c, e, 0).wait()

            @pl.when(jnp.logical_not(moves))
            def _():
                held[c, e] = jnp.zeros((span, held.shape[3]), held.dtype)

            store(c, e).start()
    for e in range(entries):
        for c in range(2):
            store(c, e).wait()


def gather_pages(kv_rows, ctx_len, migrations, page_len, page_rows):
    entries = migrations.shape[1]
    hd = kv_rows.shape[2]
    span = MAXP * page_rows
    return pl.pallas_call(
        functools.partial(gather_kernel, page_len, page_rows),
        out_shape=[jax.ShapeDtypeStruct((entries * span, hd), kv_rows.dtype)] * 2,
        in_specs=[
            pl.BlockSpec(memory_space=pltpu.SMEM),
            pl.BlockSpec(memory_space=pltpu.SMEM),
            pl.BlockSpec(memory_space=pl.ANY),
        ],
        out_specs=[pl.BlockSpec(memory_space=pl.ANY)] * 2,
        scratch_shapes=[
            pltpu.VMEM((2, entries, span, hd), kv_rows.dtype),
            pltpu.SemaphoreType.DMA((2, entries)),
            pltpu.SemaphoreType.DMA((2, entries)),
        ],
        compiler_params=pltpu.CompilerParams(vmem_limit_bytes=VMEM_BYTES),
        name="gather_pages",
    )(ctx_len, migrations, kv_rows)


def attend_kernel(
    page_len, kv_slots, group, steps, chunks, together,
    ctx_ref, q_ref, kv_ref, out_ref, pool, starts, sems,
):
    requests, rows, hd = q_ref.shape
    page_rows = page_len * kv_slots
    pool_rows = kv_ref.shape[1]
    chunk_rows = pool_rows // chunks
    span = MAXP * page_rows
    last = pool_rows - span
    scale = 1.0 / math.sqrt(hd)

    def chunk_copy(c, i):
        part = pl.ds(pl.multiple_of(i * chunk_rows, chunk_rows), chunk_rows)
        return pltpu.make_async_copy(kv_ref.at[c, part], pool.at[c, part], sems.at[c, i])

    for i in range(chunks):
        for c in range(2):
            chunk_copy(c, i).start()

    def place(i, total):
        starts[i] = total
        return total + (ctx_ref[i] + 2 + page_len - 1) // page_len * page_rows

    lax.fori_loop(0, requests, place, 0)

    def wait_chunk(i, carry):
        for c in range(2):
            chunk_copy(c, i).wait()
        return carry

    row_id = lax.broadcasted_iota(jnp.int32, (rows, span), 0)
    column = lax.broadcasted_iota(jnp.int32, (rows, span), 1)
    per_step = kv_slots * group
    step_of = row_id // per_step
    same_head = (row_id % per_step) // group == column % kv_slots
    column = column - step_of * kv_slots

    def batch(b, waited):
        tail = jnp.minimum(starts[b * together + together - 1], last) + span
        needed = (tail + chunk_rows - 1) // chunk_rows
        lax.fori_loop(waited, needed, wait_chunk, 0)
        for u in range(together):
            r = b * together + u
            start = starts[r]
            base = pl.multiple_of(jnp.minimum(start, last), page_rows)
            low = start - base
            high = low + (ctx_ref[r] + 1) * kv_slots
            keys = pool[0, pl.ds(base, span), :]
            scores = lax.dot_general(
                q_ref[r], keys, (((1,), (1,)), ((), ())), preferred_element_type=jnp.float32
            ) * scale
            valid = same_head & (column + step_of * kv_slots >= low) & (column < high)
            scores = jnp.where(valid, scores, -1e30)
            top = jnp.max(scores, axis=1, keepdims=True)
            weights = jnp.exp(scores - top)
            total = jnp.sum(weights, axis=1, keepdims=True)
            values = pool[1, pl.ds(base, span), :]
            mixed = jnp.dot(
                weights.astype(jnp.bfloat16), values, preferred_element_type=jnp.float32
            )
            out_ref[r] = (mixed / total).astype(out_ref.dtype)
        return jnp.maximum(waited, needed)

    waited = lax.fori_loop(0, requests // together, batch, 0)
    lax.fori_loop(waited, chunks, wait_chunk, 0)


def attend(kv_rows, ctx_len, query, page_len, kv_slots):
    requests, steps, width = query.shape
    hd = kv_rows.shape[2]
    heads = width // hd
    group = heads // kv_slots
    rows = steps * heads
    pool_pages = kv_rows.shape[1] // (page_len * kv_slots)
    chunks = divisor_near(pool_pages, 16)
    together = divisor_near(requests, 4)
    shaped = query.reshape(requests, rows, hd)
    out = pl.pallas_call(
        functools.partial(attend_kernel, page_len, kv_slots, group, steps, chunks, together),
        out_shape=jax.ShapeDtypeStruct((requests, rows, hd), query.dtype),
        in_specs=[
            pl.BlockSpec(memory_space=pltpu.SMEM),
            pl.BlockSpec(memory_space=pltpu.VMEM),
            pl.BlockSpec(memory_space=pl.ANY),
        ],
        out_specs=pl.BlockSpec(memory_space=pltpu.VMEM),
        scratch_shapes=[
            pltpu.VMEM(kv_rows.shape, kv_rows.dtype),
            pltpu.SMEM((requests,), jnp.int32),
            pltpu.SemaphoreType.DMA((2, chunks)),
        ],
        compiler_params=pltpu.CompilerParams(vmem_limit_bytes=VMEM_BYTES),
        cost_estimate=pl.CostEstimate(
            flops=4 * requests * rows * MAXP * page_len * kv_slots * hd,
            bytes_accessed=2 * kv_rows.size,
            transcendentals=0,
        ),
        name="paged_attention",
    )(ctx_len, shaped, kv_rows)
    return out.reshape(requests * steps, width)


def project_kernel(
    count, chunks, slots, lag,
    a_ref, w_ref, out_ref,
    w_buf, own, staged, from_left, from_right,
    w_sem, send_left, send_right, recv_left, recv_right, cast_left, cast_right, cast_in,
):
    me = lax.axis_index("tp")
    width = w_buf.shape[2]
    has_left = me > 0
    has_right = me < count - 1
    left = jnp.maximum(me - 1, 0)
    right = jnp.minimum(me + 1, count - 1)

    def weights_copy(c):
        slot = lax.rem(c, slots)
        part = pl.ds(pl.multiple_of(c * width, width), width)
        return pltpu.make_async_copy(w_ref.at[:, part], w_buf.at[slot], w_sem.at[slot])

    def columns(c):
        return pl.ds(pl.multiple_of(c * width, width), width)

    def owner_of(c):
        return count // 2 - 1 + lax.rem(c, 2)

    def reduce_right(c):
        return pltpu.make_async_remote_copy(
            src_ref=staged.at[c], dst_ref=from_left.at[c],
            send_sem=send_right.at[c], recv_sem=recv_left.at[c],
            device_id={"tp": right}, device_id_type=MESH,
        )

    def reduce_left(c):
        return pltpu.make_async_remote_copy(
            src_ref=staged.at[c], dst_ref=from_right.at[c],
            send_sem=send_left.at[c], recv_sem=recv_right.at[c],
            device_id={"tp": left}, device_id_type=MESH,
        )

    def cast_to_right(c):
        return pltpu.make_async_remote_copy(
            src_ref=out_ref.at[:, columns(c)], dst_ref=out_ref.at[:, columns(c)],
            send_sem=cast_right.at[c], recv_sem=cast_in.at[c],
            device_id={"tp": right}, device_id_type=MESH,
        )

    def cast_to_left(c):
        return pltpu.make_async_remote_copy(
            src_ref=out_ref.at[:, columns(c)], dst_ref=out_ref.at[:, columns(c)],
            send_sem=cast_left.at[c], recv_sem=cast_in.at[c],
            device_id={"tp": left}, device_id_type=MESH,
        )

    for c in range(slots):
        weights_copy(c).start()

    barrier = pltpu.get_barrier_semaphore()

    @pl.when(has_left)
    def _():
        pl.semaphore_signal(barrier, inc=1, device_id={"tp": left}, device_id_type=MESH)

    @pl.when(has_right)
    def _():
        pl.semaphore_signal(barrier, inc=1, device_id={"tp": right}, device_id_type=MESH)

    pl.semaphore_wait(barrier, has_left.astype(jnp.int32) + has_right.astype(jnp.int32))

    def forward(c):
        owner = owner_of(c)

        @pl.when(me < owner)
        def _():
            cast_to_right(c).wait_recv()

            @pl.when(has_left)
            def _():
                cast_to_left(c).start()

        @pl.when(me > owner)
        def _():
            cast_to_left(c).wait_recv()

            @pl.when(has_right)
            def _():
                cast_to_right(c).start()

    edge = jnp.logical_not(has_left & has_right)

    def send_on(c):
        @pl.when(me < owner_of(c))
        def _():
            reduce_right(c).start()

        @pl.when(me > owner_of(c))
        def _():
            reduce_left(c).start()

    def compute(c):
        slot = lax.rem(c, slots)
        weights_copy(c).wait()
        own[c] = jnp.dot(a_ref[...], w_buf[slot], preferred_element_type=jnp.float32)

        @pl.when(c + slots < chunks)
        def _():
            weights_copy(c + slots).start()

        @pl.when(edge & (me != owner_of(c)))
        def _():
            staged[c] = own[c].astype(staged.dtype)
            send_on(c)

    def relay(c):
        @pl.when(jnp.logical_not(edge) & (me < owner_of(c)))
        def _():
            reduce_right(c).wait_recv()
            staged[c] = (own[c] + from_left[c].astype(jnp.float32)).astype(staged.dtype)

        @pl.when(jnp.logical_not(edge) & (me > owner_of(c)))
        def _():
            reduce_left(c).wait_recv()
            staged[c] = (own[c] + from_right[c].astype(jnp.float32)).astype(staged.dtype)

        @pl.when(jnp.logical_not(edge))
        def _():
            send_on(c)

    def finalize(c):
        @pl.when(me == owner_of(c))
        def _():
            @pl.when(has_left)
            def _():
                reduce_right(c).wait_recv()
                own[c] = own[c] + from_left[c].astype(jnp.float32)

            @pl.when(has_right)
            def _():
                reduce_left(c).wait_recv()
                own[c] = own[c] + from_right[c].astype(jnp.float32)

            out_ref[:, columns(c)] = own[c].astype(out_ref.dtype)

            @pl.when(has_left)
            def _():
                cast_to_left(c).start()

            @pl.when(has_right)
            def _():
                cast_to_right(c).start()

    def step(t, carry):
        for stage, late in ((compute, 0), (relay, 1), (finalize, 3), (forward, lag)):
            @pl.when((t >= late) & (t < chunks + late))
            def _():
                stage(t - late)

        return carry

    lax.fori_loop(0, chunks + lag, step, 0)

    def finish(c, carry):
        owner = owner_of(c)

        @pl.when(me < owner)
        def _():
            reduce_right(c).wait_send()

        @pl.when(me > owner)
        def _():
            reduce_left(c).wait_send()

        @pl.when(has_left & (me <= owner))
        def _():
            cast_to_left(c).wait_send()

        @pl.when(has_right & (me >= owner))
        def _():
            cast_to_right(c).wait_send()

        return carry

    lax.fori_loop(0, chunks, finish, 0)


def project(attention, weight, count):
    rows, depth = attention.shape
    columns = weight.shape[1]
    width = 512 if columns % 512 == 0 else 128
    chunks = columns // width
    slots = min(4, chunks)
    lag = 6
    dma = pltpu.SemaphoreType.DMA
    return pl.pallas_call(
        functools.partial(project_kernel, count, chunks, slots, lag),
        out_shape=jax.ShapeDtypeStruct((rows, columns), attention.dtype),
        in_specs=[pl.BlockSpec(memory_space=pltpu.VMEM), pl.BlockSpec(memory_space=pl.ANY)],
        out_specs=pl.BlockSpec(memory_space=pltpu.VMEM),
        scratch_shapes=[
            pltpu.VMEM((slots, depth, width), weight.dtype),
            pltpu.VMEM((chunks, rows, width), jnp.float32),
            pltpu.VMEM((chunks, rows, width), attention.dtype),
            pltpu.VMEM((chunks, rows, width), attention.dtype),
            pltpu.VMEM((chunks, rows, width), attention.dtype),
            dma((slots,)),
        ]
        + [dma((chunks,))] * 7,
        compiler_params=pltpu.CompilerParams(
            collective_id=0, has_side_effects=True, vmem_limit_bytes=VMEM_BYTES
        ),
        cost_estimate=pl.CostEstimate(
            flops=2 * rows * depth * columns,
            bytes_accessed=2 * weight.size + 100 * 1000 * 1000,
            transcendentals=0,
        ),
        name="project_and_sum",
    )(attention, weight)


def on_device(query, kv_pool, ctx_len, migrations, o_weight):
    _, pool_size, page_len, kv_slots, hd = kv_pool.shape
    slot_count, step_count, _ = query.shape
    replicas = lax.axis_size("rep")
    count = lax.axis_size("tp")
    page_rows = page_len * kv_slots
    kv_rows = kv_pool.reshape(2, pool_size * page_rows, hd)
    lists = lax.all_gather(migrations[0, 0, 1:], "rep", axis=0)
    sends = lists[:, 1] > 0
    places = jnp.arange(replicas, dtype=jnp.int32)
    shift = jnp.max(jnp.where(sends, lists[:, 0] ^ places, 0))
    outgoing = gather_pages(kv_rows, ctx_len, migrations, page_len, page_rows)
    outgoing, shift = lax.optimization_barrier((outgoing, shift))
    far = [lax.ppermute(block, "rep", [(i, i ^ 2) for i in range(replicas)]) for block in outgoing]
    attention = attend(kv_rows, ctx_len, query, page_len, kv_slots)
    layer_out = project(attention, o_weight, count)
    far, layer_out = lax.optimization_barrier((far, layer_out))
    turned = [jnp.where(shift == 1, block, crossed) for block, crossed in zip(outgoing, far)]
    near = [lax.ppermute(block, "rep", [(i, i ^ 1) for i in range(replicas)]) for block in turned]
    source = jnp.where(migrations[0, 0, 2] > 0, 0, jnp.where(shift == 2, 1, 2))
    landed = assemble(source.reshape(1), far, near)
    arrived = landed.reshape(2, -1, page_len, kv_slots, hd)
    return (layer_out.reshape(slot_count, step_count, -1), arrived)


def assemble_kernel(parts, source_ref, far0, far1, near0, near1, out_ref, held, in_sems, out_sems):
    span = held.shape[2]
    source = source_ref[0]

    def fetch(block, c, e):
        return pltpu.make_async_copy(
            block.at[pl.ds(e * span, span)], held.at[c, e], in_sems.at[c, e]
        )

    def store(c, e):
        return pltpu.make_async_copy(
            held.at[c, e], out_ref.at[c, pl.ds(e * span, span)], out_sems.at[c, e]
        )

    for c, (straight, turned) in enumerate(((far0, near0), (far1, near1))):
        for e in range(parts):
            @pl.when(source != 2)
            def _():
                fetch(straight, c, e).start()

            @pl.when(source == 2)
            def _():
                fetch(turned, c, e).start()

    for c in range(2):
        for e in range(parts):
            fetch(far0, c, e).wait()

            @pl.when(source == 0)
            def _():
                held[c, e] = jnp.zeros(held.shape[2:], held.dtype)

            store(c, e).start()
    for c in range(2):
        for e in range(parts):
            store(c, e).wait()


def assemble(source, far, near):
    rows, hd = far[0].shape
    parts = 8
    return pl.pallas_call(
        functools.partial(assemble_kernel, parts),
        out_shape=jax.ShapeDtypeStruct((2, rows, hd), far[0].dtype),
        in_specs=[pl.BlockSpec(memory_space=pltpu.SMEM)] + [pl.BlockSpec(memory_space=pl.ANY)] * 4,
        out_specs=pl.BlockSpec(memory_space=pl.ANY),
        scratch_shapes=[
            pltpu.VMEM((2, parts, rows // parts, hd), far[0].dtype),
            pltpu.SemaphoreType.DMA((2, parts)),
            pltpu.SemaphoreType.DMA((2, parts)),
        ],
        compiler_params=pltpu.CompilerParams(vmem_limit_bytes=VMEM_BYTES),
        name="assemble",
    )(source, *far, *near)


def solution(mesh):
    return jax.shard_map(
        on_device,
        mesh=mesh,
        in_specs=(
            P(("grp", "rep"), None, "tp"),
            P(None, ("grp", "rep"), None, "tp", None),
            P(("grp", "rep")),
            P(("grp", "rep"), None, None),
            P("tp", None),
        ),
        out_specs=(P(("grp", "rep"), None, None), P(None, ("grp", "rep"), None, "tp", None)),
        check_vma=False,
    )
```

```python
import functools
import math

import jax
import jax.numpy as jnp
from jax import lax
from jax.experimental import pallas as pl
from jax.experimental.pallas import tpu as pltpu
from jax.sharding import PartitionSpec as P

MAXP = 4
MESH = pl.DeviceIdType.MESH
VMEM_BYTES = 60 * 1024 * 1024


def divisor_near(total, most):
    for parts in range(min(most, total), 0, -1):
        if total % parts == 0:
            return parts
    return 1


def gather_kernel(page_len, page_rows, ctx_ref, mig_ref, kv_ref, *refs):
    outs, (held, in_sems, out_sems) = refs[:2], refs[2:]
    entries = mig_ref.shape[1]
    span = MAXP * page_rows
    last = kv_ref.shape[1] - span

    def first_row(slot):
        def add(i, total):
            return total + (ctx_ref[i] + 2 + page_len - 1) // page_len

        return lax.fori_loop(0, slot, add, 0) * page_rows

    def fetch(c, e, row):
        return pltpu.make_async_copy(
            kv_ref.at[c, pl.ds(pl.multiple_of(row, page_rows), span)],
            held.at[c, e],
            in_sems.at[c, e],
        )

    def store(c, e):
        return pltpu.make_async_copy(
            held.at[c, e], outs[c].at[pl.ds(e * span, span)], out_sems.at[c, e]
        )

    for e in range(entries):
        row = jnp.minimum(first_row(mig_ref[0, e, 0]), last)
        for c in range(2):
            fetch(c, e, row).start()
    for e in range(entries):
        moves = mig_ref[0, e, 2] > 0
        for c in range(2):
            fetch(c, e, 0).wait()

            @pl.when(jnp.logical_not(moves))
            def _():
                held[c, e] = jnp.zeros((span, held.shape[3]), held.dtype)

            store(c, e).start()
    for e in range(entries):
        for c in range(2):
            store(c, e).wait()


def gather_pages(kv_rows, ctx_len, migrations, page_len, page_rows):
    entries = migrations.shape[1]
    hd = kv_rows.shape[2]
    span = MAXP * page_rows
    return pl.pallas_call(
        functools.partial(gather_kernel, page_len, page_rows),
        out_shape=[jax.ShapeDtypeStruct((entries * span, hd), kv_rows.dtype)] * 2,
        in_specs=[
            pl.BlockSpec(memory_space=pltpu.SMEM),
            pl.BlockSpec(memory_space=pltpu.SMEM),
            pl.BlockSpec(memory_space=pl.ANY),
        ],
        out_specs=[pl.BlockSpec(memory_space=pl.ANY)] * 2,
        scratch_shapes=[
            pltpu.VMEM((2, entries, span, hd), kv_rows.dtype),
            pltpu.SemaphoreType.DMA((2, entries)),
            pltpu.SemaphoreType.DMA((2, entries)),
        ],
        compiler_params=pltpu.CompilerParams(vmem_limit_bytes=VMEM_BYTES),
        name="gather_pages",
    )(ctx_len, migrations, kv_rows)


def attend_kernel(
    page_len, kv_slots, group, steps, chunks, together,
    ctx_ref, q_ref, kv_ref, out_ref, pool, starts, sems,
):
    requests, rows, hd = q_ref.shape
    page_rows = page_len * kv_slots
    pool_rows = kv_ref.shape[1]
    chunk_rows = pool_rows // chunks
    span = MAXP * page_rows
    last = pool_rows - span
    scale = 1.0 / math.sqrt(hd)

    def chunk_copy(c, i):
        part = pl.ds(pl.multiple_of(i * chunk_rows, chunk_rows), chunk_rows)
        return pltpu.make_async_copy(kv_ref.at[c, part], pool.at[c, part], sems.at[c, i])

    for i in range(chunks):
        for c in range(2):
            chunk_copy(c, i).start()

    def place(i, total):
        starts[i] = total
        return total + (ctx_ref[i] + 2 + page_len - 1) // page_len * page_rows

    lax.fori_loop(0, requests, place, 0)

    def wait_chunk(i, carry):
        for c in range(2):
            chunk_copy(c, i).wait()
        return carry

    row_id = lax.broadcasted_iota(jnp.int32, (rows, span), 0)
    column = lax.broadcasted_iota(jnp.int32, (rows, span), 1)
    per_step = kv_slots * group
    step_of = row_id // per_step
    same_head = (row_id % per_step) // group == column % kv_slots
    column = column - step_of * kv_slots

    def batch(b, waited):
        tail = jnp.minimum(starts[b * together + together - 1], last) + span
        needed = (tail + chunk_rows - 1) // chunk_rows
        lax.fori_loop(waited, needed, wait_chunk, 0)
        for u in range(together):
            r = b * together + u
            start = starts[r]
            base = pl.multiple_of(jnp.minimum(start, last), page_rows)
            low = start - base
            high = low + (ctx_ref[r] + 1) * kv_slots
            keys = pool[0, pl.ds(base, span), :]
            scores = lax.dot_general(
                q_ref[r], keys, (((1,), (1,)), ((), ())), preferred_element_type=jnp.float32
            ) * scale
            valid = same_head & (column + step_of * kv_slots >= low) & (column < high)
            scores = jnp.where(valid, scores, -1e30)
            top = jnp.max(scores, axis=1, keepdims=True)
            weights = jnp.exp(scores - top)
            total = jnp.sum(weights, axis=1, keepdims=True)
            values = pool[1, pl.ds(base, span), :]
            mixed = jnp.dot(
                weights.astype(jnp.bfloat16), values, preferred_element_type=jnp.float32
            )
            out_ref[r] = (mixed / total).astype(out_ref.dtype)
        return jnp.maximum(waited, needed)

    waited = lax.fori_loop(0, requests // together, batch, 0)
    lax.fori_loop(waited, chunks, wait_chunk, 0)


def attend(kv_rows, ctx_len, query, page_len, kv_slots):
    requests, steps, width = query.shape
    hd = kv_rows.shape[2]
    heads = width // hd
    group = heads // kv_slots
    rows = steps * heads
    pool_pages = kv_rows.shape[1] // (page_len * kv_slots)
    chunks = divisor_near(pool_pages, 16)
    together = divisor_near(requests, 4)
    shaped = query.reshape(requests, rows, hd)
    out = pl.pallas_call(
        functools.partial(attend_kernel, page_len, kv_slots, group, steps, chunks, together),
        out_shape=jax.ShapeDtypeStruct((requests, rows, hd), query.dtype),
        in_specs=[
            pl.BlockSpec(memory_space=pltpu.SMEM),
            pl.BlockSpec(memory_space=pltpu.VMEM),
            pl.BlockSpec(memory_space=pl.ANY),
        ],
        out_specs=pl.BlockSpec(memory_space=pltpu.VMEM),
        scratch_shapes=[
            pltpu.VMEM(kv_rows.shape, kv_rows.dtype),
            pltpu.SMEM((requests,), jnp.int32),
            pltpu.SemaphoreType.DMA((2, chunks)),
        ],
        compiler_params=pltpu.CompilerParams(vmem_limit_bytes=VMEM_BYTES),
        cost_estimate=pl.CostEstimate(
            flops=4 * requests * rows * MAXP * page_len * kv_slots * hd,
            bytes_accessed=2 * kv_rows.size,
            transcendentals=0,
        ),
        name="paged_attention",
    )(ctx_len, shaped, kv_rows)
    return out.reshape(requests * steps, width)


def project_kernel(
    count, chunks, slots, lag,
    a_ref, w_ref, out_ref,
    w_buf, own, staged, from_left, from_right,
    w_sem, send_left, send_right, recv_left, recv_right, cast_left, cast_right, cast_in,
):
    me = lax.axis_index("tp")
    width = w_buf.shape[2]
    has_left = me > 0
    has_right = me < count - 1
    left = jnp.maximum(me - 1, 0)
    right = jnp.minimum(me + 1, count - 1)

    def weights_copy(c):
        slot = lax.rem(c, slots)
        part = pl.ds(pl.multiple_of(c * width, width), width)
        return pltpu.make_async_copy(w_ref.at[:, part], w_buf.at[slot], w_sem.at[slot])

    def columns(c):
        return pl.ds(pl.multiple_of(c * width, width), width)

    def owner_of(c):
        return count // 2 - 1 + lax.rem(c, 2)

    def reduce_right(c):
        return pltpu.make_async_remote_copy(
            src_ref=staged.at[c], dst_ref=from_left.at[c],
            send_sem=send_right.at[c], recv_sem=recv_left.at[c],
            device_id={"tp": right}, device_id_type=MESH,
        )

    def reduce_left(c):
        return pltpu.make_async_remote_copy(
            src_ref=staged.at[c], dst_ref=from_right.at[c],
            send_sem=send_left.at[c], recv_sem=recv_right.at[c],
            device_id={"tp": left}, device_id_type=MESH,
        )

    def cast_to_right(c):
        return pltpu.make_async_remote_copy(
            src_ref=out_ref.at[:, columns(c)], dst_ref=out_ref.at[:, columns(c)],
            send_sem=cast_right.at[c], recv_sem=cast_in.at[c],
            device_id={"tp": right}, device_id_type=MESH,
        )

    def cast_to_left(c):
        return pltpu.make_async_remote_copy(
            src_ref=out_ref.at[:, columns(c)], dst_ref=out_ref.at[:, columns(c)],
            send_sem=cast_left.at[c], recv_sem=cast_in.at[c],
            device_id={"tp": left}, device_id_type=MESH,
        )

    for c in range(slots):
        weights_copy(c).start()

    barrier = pltpu.get_barrier_semaphore()

    @pl.when(has_left)
    def _():
        pl.semaphore_signal(barrier, inc=1, device_id={"tp": left}, device_id_type=MESH)

    @pl.when(has_right)
    def _():
        pl.semaphore_signal(barrier, inc=1, device_id={"tp": right}, device_id_type=MESH)

    pl.semaphore_wait(barrier, has_left.astype(jnp.int32) + has_right.astype(jnp.int32))

    def forward(c):
        owner = owner_of(c)

        @pl.when(me < owner)
        def _():
            cast_to_right(c).wait_recv()

            @pl.when(has_left)
            def _():
                cast_to_left(c).start()

        @pl.when(me > owner)
        def _():
            cast_to_left(c).wait_recv()

            @pl.when(has_right)
            def _():
                cast_to_right(c).start()

    edge = jnp.logical_not(has_left & has_right)

    def send_on(c):
        @pl.when(me < owner_of(c))
        def _():
            reduce_right(c).start()

        @pl.when(me > owner_of(c))
        def _():
            reduce_left(c).start()

    def compute(c):
        slot = lax.rem(c, slots)
        weights_copy(c).wait()
        own[c] = jnp.dot(a_ref[...], w_buf[slot], preferred_element_type=jnp.float32)

        @pl.when(c + slots < chunks)
        def _():
            weights_copy(c + slots).start()

        @pl.when(edge & (me != owner_of(c)))
        def _():
            staged[c] = own[c].astype(staged.dtype)
            send_on(c)

    def relay(c):
        @pl.when(jnp.logical_not(edge) & (me < owner_of(c)))
        def _():
            reduce_right(c).wait_recv()
            staged[c] = (own[c] + from_left[c].astype(jnp.float32)).astype(staged.dtype)

        @pl.when(jnp.logical_not(edge) & (me > owner_of(c)))
        def _():
            reduce_left(c).wait_recv()
            staged[c] = (own[c] + from_right[c].astype(jnp.float32)).astype(staged.dtype)

        @pl.when(jnp.logical_not(edge))
        def _():
            send_on(c)

    def finalize(c):
        @pl.when(me == owner_of(c))
        def _():
            @pl.when(has_left)
            def _():
                reduce_right(c).wait_recv()
                own[c] = own[c] + from_left[c].astype(jnp.float32)

            @pl.when(has_right)
            def _():
                reduce_left(c).wait_recv()
                own[c] = own[c] + from_right[c].astype(jnp.float32)

            out_ref[:, columns(c)] = own[c].astype(out_ref.dtype)

            @pl.when(has_left)
            def _():
                cast_to_left(c).start()

            @pl.when(has_right)
            def _():
                cast_to_right(c).start()

    def step(t, carry):
        for stage, late in ((compute, 0), (relay, 1), (finalize, 3), (forward, lag)):
            @pl.when((t >= late) & (t < chunks + late))
            def _():
                stage(t - late)

        return carry

    lax.fori_loop(0, chunks + lag, step, 0)

    def finish(c, carry):
        owner = owner_of(c)

        @pl.when(me < owner)
        def _():
            reduce_right(c).wait_send()

        @pl.when(me > owner)
        def _():
            reduce_left(c).wait_send()

        @pl.when(has_left & (me <= owner))
        def _():
            cast_to_left(c).wait_send()

        @pl.when(has_right & (me >= owner))
        def _():
            cast_to_right(c).wait_send()

        return carry

    lax.fori_loop(0, chunks, finish, 0)


def project(attention, weight, count):
    rows, depth = attention.shape
    columns = weight.shape[1]
    width = 512 if columns % 512 == 0 else 128
    chunks = columns // width
    slots = min(4, chunks)
    lag = 6
    dma = pltpu.SemaphoreType.DMA
    return pl.pallas_call(
        functools.partial(project_kernel, count, chunks, slots, lag),
        out_shape=jax.ShapeDtypeStruct((rows, columns), attention.dtype),
        in_specs=[pl.BlockSpec(memory_space=pltpu.VMEM), pl.BlockSpec(memory_space=pl.ANY)],
        out_specs=pl.BlockSpec(memory_space=pltpu.VMEM),
        scratch_shapes=[
            pltpu.VMEM((slots, depth, width), weight.dtype),
            pltpu.VMEM((chunks, rows, width), jnp.float32),
            pltpu.VMEM((chunks, rows, width), attention.dtype),
            pltpu.VMEM((chunks, rows, width), attention.dtype),
            pltpu.VMEM((chunks, rows, width), attention.dtype),
            dma((slots,)),
        ]
        + [dma((chunks,))] * 7,
        compiler_params=pltpu.CompilerParams(
            collective_id=0, has_side_effects=True, vmem_limit_bytes=VMEM_BYTES
        ),
        cost_estimate=pl.CostEstimate(
            flops=2 * rows * depth * columns,
            bytes_accessed=2 * weight.size + 100 * 1000 * 1000,
            transcendentals=0,
        ),
        name="project_and_sum",
    )(attention, weight)


def on_device(query, kv_pool, ctx_len, migrations, o_weight):
    _, pool_size, page_len, kv_slots, hd = kv_pool.shape
    slot_count, step_count, _ = query.shape
    replicas = lax.axis_size("rep")
    count = lax.axis_size("tp")
    page_rows = page_len * kv_slots
    kv_rows = kv_pool.reshape(2, pool_size * page_rows, hd)
    own = lax.axis_index("rep")
    shift = jnp.where(migrations[0, 0, 2] > 0, migrations[0, 0, 1] ^ own, 0).reshape(1, 1)
    for hop in (2, 1):
        other = lax.ppermute(shift, "rep", [(i, i ^ hop) for i in range(replicas)])
        shift = jnp.maximum(shift, other)
    shift = shift[0, 0]
    outgoing = gather_pages(kv_rows, ctx_len, migrations, page_len, page_rows)
    outgoing, shift = lax.optimization_barrier((outgoing, shift))
    far = [lax.ppermute(block, "rep", [(i, i ^ 2) for i in range(replicas)]) for block in outgoing]
    attention = attend(kv_rows, ctx_len, query, page_len, kv_slots)
    layer_out = project(attention, o_weight, count)
    far, layer_out = lax.optimization_barrier((far, layer_out))
    turned = [jnp.where(shift == 1, block, crossed) for block, crossed in zip(outgoing, far)]
    near = [lax.ppermute(block, "rep", [(i, i ^ 1) for i in range(replicas)]) for block in turned]
    source = jnp.where(migrations[0, 0, 2] > 0, 0, jnp.where(shift == 2, 1, 2))
    landed = assemble(source.reshape(1), far, near)
    arrived = landed.reshape(2, -1, page_len, kv_slots, hd)
    return (layer_out.reshape(slot_count, step_count, -1), arrived)


def assemble_kernel(parts, source_ref, far0, far1, near0, near1, out_ref, held, in_sems, out_sems):
    span = held.shape[2]
    source = source_ref[0]

    def fetch(block, c, e):
        return pltpu.make_async_copy(
            block.at[pl.ds(e * span, span)], held.at[c, e], in_sems.at[c, e]
        )

    def store(c, e):
        return pltpu.make_async_copy(
            held.at[c, e], out_ref.at[c, pl.ds(e * span, span)], out_sems.at[c, e]
        )

    for c, (straight, turned) in enumerate(((far0, near0), (far1, near1))):
        for e in range(parts):
            @pl.when(source != 2)
            def _():
                fetch(straight, c, e).start()

            @pl.when(source == 2)
            def _():
                fetch(turned, c, e).start()

    for c in range(2):
        for e in range(parts):
            fetch(far0, c, e).wait()

            @pl.when(source == 0)
            def _():
                held[c, e] = jnp.zeros(held.shape[2:], held.dtype)

            store(c, e).start()
    for c in range(2):
        for e in range(parts):
            store(c, e).wait()


def assemble(source, far, near):
    rows, hd = far[0].shape
    parts = 8
    return pl.pallas_call(
        functools.partial(assemble_kernel, parts),
        out_shape=jax.ShapeDtypeStruct((2, rows, hd), far[0].dtype),
        in_specs=[pl.BlockSpec(memory_space=pltpu.SMEM)] + [pl.BlockSpec(memory_space=pl.ANY)] * 4,
        out_specs=pl.BlockSpec(memory_space=pl.ANY),
        scratch_shapes=[
            pltpu.VMEM((2, parts, rows // parts, hd), far[0].dtype),
            pltpu.SemaphoreType.DMA((2, parts)),
            pltpu.SemaphoreType.DMA((2, parts)),
        ],
        compiler_params=pltpu.CompilerParams(vmem_limit_bytes=VMEM_BYTES),
        name="assemble",
    )(source, *far, *near)


def solution(mesh):
    return jax.shard_map(
        on_device,
        mesh=mesh,
        in_specs=(
            P(("grp", "rep"), None, "tp"),
            P(None, ("grp", "rep"), None, "tp", None),
            P(("grp", "rep")),
            P(("grp", "rep"), None, None),
            P("tp", None),
        ),
        out_specs=(P(("grp", "rep"), None, None), P(None, ("grp", "rep"), None, "tp", None)),
        check_vma=False,
    )
```
